32 devices in a mesh: section: 4 (over y, core), dom: 8 (over z, x).
Axes of the slice: x: 2, y: 2, z: 4, core: 2. Of those that a mesh axis runs over, the one named last changes fastest.
Arguments:
- carry_h: bfloat16 [4, 8192, 512], P('section', 'dom'), may hold values from -6 to 6
- carry_h0: bfloat16 [4, 8192, 512], P('section', 'dom'), may hold values from -6 to 6
- new_h0: bfloat16 [3, 8192, 512], P(None, 'dom'), may hold values from -6 to 6
- weights: bfloat16 [4, 512, 512], P('section'), may hold values from -0.25 to 0.25
- adj_blocks: bfloat16 [64, 24, 128, 128], P('dom'), may hold values from -0.109375 to 0.109375
- col_index: int32 [64, 24], P('dom'), may hold values from 0 to 15
- counts: int32 [64], P('dom'), may hold values from 1 to 24, as said below
- send_list: int32 [8, 8], replicated, may hold values from 0 to 7
Outputs:
- layer_out: bfloat16 [4, 4, 8192, 512], P('section', None, 'dom')
The draws below stay inside these ranges and needn't reach their ends.
Inputs may be any that keep to these rules, and one draw needn't show every extreme that they name: `counts`: every graph part has a row block with exactly 24 live blocks; parts differ in their mean load.
All inputs are finite; a program needn't handle non-finite values.
Results may differ from the reference program's by a relative error of at most 0.0052.
Values may be sent and summed in bfloat16 or wider, within the bound.
No kernel may reach another device: no remote copies, remote signals or barrier semaphores. Data moves between devices by JAX's collectives and lax.ppermute only.
A program may use at most 128 MiB of HBM per device.

```python
import math
import jax
import jax.numpy as jnp
from jax import lax

D = 512
ROWS_DEV = 1024
BLOCK = 128
SLOTS = 24
STEPS = 4
NEW_GROUPS = 3
GROUP = 8192
RBLOCKS = 64
TABLE = 16
N_SECTION = 4
N_DOM = 8


def draw_counts(key, part):
    per_part = ROWS_DEV // BLOCK
    total = per_part * N_DOM
    ceiling = jax.random.randint(jax.random.fold_in(key, 11), (N_DOM,), SLOTS // 2, SLOTS + 1)
    raw_draw = jax.random.randint(jax.random.fold_in(key, 12), (total,), 0, 1 << 20)
    owner_part = jnp.arange(total) // per_part
    drawn = 1 + raw_draw % ceiling[owner_part]
    chosen = jax.random.randint(jax.random.fold_in(key, 13), (N_DOM,), 0, per_part)
    full_row = jnp.arange(total) % per_part == chosen[owner_part]
    return jnp.where(full_row, SLOTS, drawn).astype(jnp.int32)


def set_ends(result, stream_key, least, largest):
    longest = result.shape.index(max(result.shape))
    spots = []
    for shift in (0, 1):
        where = [jax.random.randint(jax.random.fold_in(stream_key, axis), (), 0, length) for axis, length in enumerate(result.shape)]
        where[longest] = (where[longest] + shift) % result.shape[longest]
        spots.append(tuple(where))
    return result.at[spots[0]].set(least).at[spots[1]].set(largest)


def level_of(rng, shape, shards, low, top_value):
    def one(axis_at, shards_of):
        draws = jax.random.uniform(jax.random.fold_in(jax.random.fold_in(rng, 6), axis_at), (shards_of,), jnp.float32, low / len(shards), top_value / len(shards))
        return jnp.repeat(jnp.exp(draws), shape[axis_at] // shards_of).reshape((-1,) + (1,) * (len(shape) - axis_at - 1))

    level = one(*shards[0])
    for cut in shards[1:]:
        level = level * one(*cut)
    return level


def normal_values(own_key, dims, deviation, reach, cuts=(), kind=jnp.bfloat16):
    array = deviation * jax.random.normal(own_key, dims, jnp.float32)
    if cuts:
        array = array * level_of(own_key, dims, cuts, -0.22, 0.18)
    return jnp.clip(array, -reach, reach).astype(kind)


def setup_inputs(seed: int = 0) -> dict:
    keys = jax.random.split(jax.random.key(seed), 9)
    return {
        "carry_h": normal_values(keys[0], (N_SECTION, GROUP, D), 1.0, 6.0, ((0, 4), (1, 8))),
        "carry_h0": normal_values(keys[1], (N_SECTION, GROUP, D), 1.0, 6.0, ((0, 4), (1, 8))),
        "new_h0": normal_values(keys[2], (NEW_GROUPS, GROUP, D), 1.0, 6.0, ((1, 8),)),
        "weights": normal_values(keys[3], (N_SECTION, D, D), D ** -0.5, 0.25, ((0, 4),)),
        "adj_blocks": normal_values(keys[4], (RBLOCKS, SLOTS, BLOCK, BLOCK), (SLOTS * BLOCK) ** -0.5, 0.109375, ((0, 8),)),
        "col_index": set_ends(jax.random.randint(keys[5], (RBLOCKS, SLOTS), 0, TABLE), jax.random.fold_in(keys[5], 1), 0, TABLE - 1).astype(jnp.int32),
        "counts": draw_counts(jax.random.fold_in(keys[8], 71), 0),
        "send_list": set_ends(jax.random.randint(keys[7], (N_DOM, N_DOM), 0, ROWS_DEV // BLOCK), jax.random.fold_in(keys[7], 1), 0, (ROWS_DEV // BLOCK) - 1).astype(jnp.int32),
    }


teleport = 0.2
strength = 1.5


def apply_layer(current, anchor, weight, beta, adj_blocks, col_index, counts, send_list):
    per_part = ROWS_DEV // BLOCK
    blocks = current.reshape(N_DOM, per_part, BLOCK, D)
    incoming = blocks[jnp.arange(N_DOM)[None, :], send_list.T]
    tables = jnp.concatenate([blocks, incoming], axis=1)

    def row_block(inputs):
        adj_one, cols, live_count, row_id = inputs
        lookup = lax.dynamic_index_in_dim(tables, (row_id // per_part).astype(jnp.int32), 0, keepdims=False)
        picked = jnp.take(lookup, cols, axis=0)
        live_slots = jnp.arange(SLOTS) < live_count
        masked = jnp.where(live_slots[:, None, None], adj_one, jnp.zeros((), adj_one.dtype))
        return jnp.einsum("kij,kjd->id", masked.astype(jnp.float32), picked.astype(jnp.float32))

    row_ids = jnp.arange(RBLOCKS).astype(jnp.int32)
    gathered = lax.map(row_block, (adj_blocks, col_index, counts, row_ids)).reshape(GROUP, D)
    mixture = ((1.0 - teleport) * gathered + teleport * anchor.astype(jnp.float32)).astype(jnp.bfloat16)
    product = jnp.dot(mixture, weight, preferred_element_type=jnp.float32)
    return jax.nn.relu((1.0 - beta) * mixture.astype(jnp.float32) + beta * product).astype(jnp.bfloat16)


def reference(carry_h, carry_h0, new_h0, weights, adj_blocks, col_index, counts, send_list):
    history = []
    for step in range(STEPS):
        current_row = []
        for layer in range(N_SECTION):
            if step == 0:
                current = carry_h[layer]
            elif layer == 0:
                current = new_h0[step - 1]
            else:
                current = history[step - 1][layer - 1]
            if step <= layer:
                anchor = carry_h0[layer - step]
            else:
                anchor = new_h0[step - layer - 1]
            layer_beta = math.log(1.0 + strength / (layer + 1))
            current_row.append(apply_layer(current, anchor, weights[layer], layer_beta, adj_blocks, col_index, counts, send_list))
        history.append(current_row)
    return jnp.stack([jnp.stack([history[step][layer] for step in range(STEPS)]) for layer in range(N_SECTION)])
```

```python
import jax
import jax.numpy as jnp
from jax import lax
from jax.experimental import pallas as pl
from jax.experimental.pallas import tpu as pltpu
from jax.sharding import PartitionSpec as P

STEPS = 4
TILE = 256

teleport = 0.2
strength = 1.5

VMEM = pl.BlockSpec(memory_space=pltpu.VMEM)
SMEM = pl.BlockSpec(memory_space=pltpu.SMEM)
ANY = pl.BlockSpec(memory_space=pl.ANY)
LIMIT = pltpu.CompilerParams(vmem_limit_bytes=24 * 2**20)


def send_kernel(ids, blocks, outgoing, sems):
    copies = [
        pltpu.make_async_copy(blocks.at[ids[q]], outgoing.at[q], sems.at[q])
        for q in range(outgoing.shape[0])
    ]
    for copy in copies:
        copy.start()
    for copy in copies:
        copy.wait()


def first_outgoing(ids, blocks):
    return pl.pallas_call(
        send_kernel,
        out_shape=jax.ShapeDtypeStruct((ids.shape[0],) + blocks.shape[1:], blocks.dtype),
        in_specs=[SMEM, ANY],
        out_specs=ANY,
        scratch_shapes=[pltpu.SemaphoreType.DMA((ids.shape[0],))],
    )(ids, blocks)


def merge_kernel(col, counts, adj, own, other, total):
    row = pl.program_id(0)
    block = adj.shape[-1]
    total[...] = jnp.zeros_like(total)

    def add(k, carry):
        total[col[row, k]] += adj[0, k].astype(jnp.float32)
        return carry

    lax.fori_loop(0, counts[row], add, 0)
    mine = own.shape[1] // block
    for entry in range(total.shape[0]):
        value = total[entry].astype(own.dtype)
        if entry < mine:
            own[:, entry * block : (entry + 1) * block] = value
        else:
            at = (entry - mine) * block
            other[:, at : at + block] = value


def merged(col, counts, adj, table):
    rows, slots, block, _ = adj.shape
    return pl.pallas_call(
        merge_kernel,
        grid=(rows,),
        out_shape=[
            jax.ShapeDtypeStruct((rows * block, rows * block), adj.dtype),
            jax.ShapeDtypeStruct((rows * block, (table - rows) * block), adj.dtype),
        ],
        in_specs=[SMEM, SMEM, pl.BlockSpec((1, slots, block, block), lambda r: (r, 0, 0, 0))],
        out_specs=[
            pl.BlockSpec((block, rows * block), lambda r: (r, 0)),
            pl.BlockSpec((block, (table - rows) * block), lambda r: (r, 0)),
        ],
        scratch_shapes=[pltpu.VMEM((table, block, block), jnp.float32)],
        compiler_params=LIMIT,
    )(col, counts, adj)


def own_kernel(flags, current, fresh, carried, new_h0, adj, partial, x, h0, sems):
    def pull(source, target, sem):
        copy = pltpu.make_async_copy(source, target, sem)
        copy.start()
        copy.wait()

    @pl.when(flags[0] == 1)
    def _():
        pull(fresh, x, sems.at[0])

    @pl.when(flags[0] == 0)
    def _():
        pull(current, x, sems.at[0])

    @pl.when(flags[1] == 1)
    def _():
        pull(new_h0.at[flags[2]], h0, sems.at[1])

    @pl.when(flags[1] == 0)
    def _():
        pull(carried, h0, sems.at[1])

    for at in range(0, x.shape[0], TILE):
        rows = slice(at, at + TILE)
        agg = jnp.dot(adj[rows], x[...], preferred_element_type=jnp.float32)
        partial[rows] = (1.0 - teleport) * agg + teleport * h0[rows].astype(jnp.float32)


def own_part(flags, current, fresh, carried, new_h0, adj):
    return pl.pallas_call(
        own_kernel,
        out_shape=jax.ShapeDtypeStruct(current.shape, jnp.float32),
        in_specs=[SMEM, ANY, ANY, ANY, ANY, VMEM],
        out_specs=VMEM,
        scratch_shapes=[
            pltpu.VMEM(current.shape, current.dtype),
            pltpu.VMEM(current.shape, current.dtype),
            pltpu.SemaphoreType.DMA((2,)),
        ],
        compiler_params=LIMIT,
    )(flags, current, fresh, carried, new_h0, adj)


def layer_kernel(last, flags, ids, beta, incoming, adj, partial, weight, fresh, *rest):
    out = rest[0]
    for at in range(0, out.shape[0], TILE):
        rows = slice(at, at + TILE)
        agg = jnp.dot(adj[rows], incoming[...], preferred_element_type=jnp.float32)
        mixture = (partial[rows] + (1.0 - teleport) * agg).astype(jnp.bfloat16)
        product = jnp.dot(mixture, weight[...], preferred_element_type=jnp.float32)
        value = (1.0 - beta[0]) * mixture.astype(jnp.float32) + beta[0] * product
        out[rows] = jnp.maximum(value, 0.0).astype(out.dtype)
    if last:
        return
    outgoing, sems = rest[1:]
    block = outgoing.shape[1]

    def send(source):
        copies = [
            pltpu.make_async_copy(
                source.at[pl.ds(pl.multiple_of(ids[q] * block, block), block)], outgoing.at[q], sems.at[q]
            )
            for q in range(outgoing.shape[0])
        ]
        for copy in copies:
            copy.start()
        for copy in copies:
            copy.wait()

    @pl.when(flags[0] == 1)
    def _():
        send(fresh)

    @pl.when(flags[0] == 0)
    def _():
        send(out)


def layer(last, flags, ids, beta, incoming, adj, partial, weight, fresh):
    parts, block, width = incoming.shape
    shapes = [jax.ShapeDtypeStruct(partial.shape, incoming.dtype)]
    if not last:
        shapes.append(jax.ShapeDtypeStruct(incoming.shape, incoming.dtype))
    return pl.pallas_call(
        lambda *refs: layer_kernel(last, *refs),
        out_shape=shapes,
        in_specs=[SMEM, SMEM, SMEM, VMEM, VMEM, VMEM, VMEM, ANY],
        out_specs=[VMEM, ANY][: len(shapes)],
        scratch_shapes=[] if last else [pltpu.SemaphoreType.DMA((parts,))],
        compiler_params=LIMIT,
    )(flags, ids, beta, incoming.reshape(parts * block, width), adj, partial, weight, fresh)


def moved(value, by):
    length = lax.axis_size("section")
    if by % length == 0:
        return value
    return lax.ppermute(value, "section", [((i + by) % length, i) for i in range(length)])


def body(carry_h, carry_h0, new_h0, weights, adj_blocks, col_index, counts, send_list):
    section = lax.axis_index("section")
    sections = lax.axis_size("section")
    row_count, width = carry_h.shape[1:]
    block_count, _, block, _ = adj_blocks.shape
    parts = send_list.shape[0]
    ids = lax.dynamic_index_in_dim(send_list, lax.axis_index("dom"), 0, keepdims=False)
    layers = (section + jnp.arange(STEPS + 1, dtype=jnp.int32)) % sections
    betas = jnp.log(1.0 + strength / (layers.astype(jnp.float32) + 1.0))
    wrapped = (section + jnp.arange(STEPS + 1, dtype=jnp.int32) >= sections).astype(jnp.int32)
    starts = (layers == 0).astype(jnp.int32).at[0].set(0)
    source = jnp.clip(sections - section - 1, 0, new_h0.shape[0] - 1)
    flags = [jnp.stack([starts[t], wrapped[t], source]) for t in range(STEPS + 1)]

    outgoing = first_outgoing(ids, carry_h[0].reshape(block_count, block, width))
    current = carry_h[0]
    layer_weights = [moved(weights[0], t) for t in range(STEPS)]
    own_adj = None
    results = []
    for t in range(STEPS):
        last = t == STEPS - 1
        incoming = lax.all_to_all(outgoing, "dom", split_axis=0, concat_axis=0, tiled=True)
        if own_adj is None:
            own_adj, other_adj = merged(col_index, counts, adj_blocks, block_count + parts)
        partial = own_part(flags[t], current, new_h0[max(t - 1, 0)], carry_h0[0], new_h0, own_adj)
        made = layer(
            last, flags[t + 1], ids, betas[t : t + 1], incoming, other_adj, partial, layer_weights[t],
            new_h0[min(t, new_h0.shape[0] - 1)],
        )
        current = made[0]
        if not last:
            outgoing = made[1]
        results.append(moved(current, -t))
    return jnp.stack(results)[None]


def solution(mesh):
    in_specs = (
        P("section", "dom", None),
        P("section", "dom", None),
        P(None, "dom", None),
        P("section", None, None),
        P("dom", None, None, None),
        P("dom", None),
        P("dom"),
        P(),
    )
    out_specs = P("section", None, "dom", None)
    return jax.shard_map(body, mesh=mesh, in_specs=in_specs, out_specs=out_specs, check_vma=False)
```

```python
import jax
import jax.numpy as jnp
from jax import lax
from jax.experimental import pallas as pl
from jax.experimental.pallas import tpu as pltpu
from jax.sharding import PartitionSpec as P

STEPS = 4
TILE = 256

teleport = 0.2
strength = 1.5

PART, SOURCE, STARTS, WRAPPED, IDS = 0, 1, 2, 2 + STEPS, 2 + 2 * STEPS

VMEM = pl.BlockSpec(memory_space=pltpu.VMEM)
SMEM = pl.BlockSpec(memory_space=pltpu.SMEM)
HBM = pl.BlockSpec(memory_space=pltpu.HBM)
LIMIT = pltpu.CompilerParams(vmem_limit_bytes=16 * 2**20)


def fast(value):
    return pltpu.with_memory_space_constraint(value, pltpu.VMEM)


def far(value):
    return pltpu.with_memory_space_constraint(value, pltpu.HBM)


def run(copies):
    for copy in copies:
        copy.start()
    for copy in copies:
        copy.wait()


def relays(parts):
    quarter = parts // 4
    if quarter == 0:
        return {}
    hops = {}
    for k in range(2 * quarter, 3 * quarter):
        across = k - 2 * quarter
        hops[k] = (quarter + across, 3 * quarter) if across % 2 == 0 else (3 * quarter + across, quarter)
    return hops


def bundles(parts):
    via = {}
    for k, (first, _) in relays(parts).items():
        via.setdefault(first, []).append(k)
    order = sorted(via) + [k for k in range(1, parts) if k not in via and k not in relays(parts)]
    return [(hop, [hop] + via.get(hop, [])) for hop in order]


def swapped(value, offset):
    parts = lax.axis_size("dom")
    return lax.ppermute(value, "dom", [(i, i ^ offset) for i in range(parts)])


def exchanged(sent, parts):
    hops = relays(parts)
    arrays, offsets = [], []
    for (hop, carried), value in zip(bundles(parts), sent):
        got = swapped(value, hop)
        arrays.append(got)
        offsets.append(hop)
        for place, k in enumerate(carried[1:], 1):
            arrays.append(swapped(got[place : place + 1], hops[k][1]))
            offsets.append(k)
    return arrays, offsets


def pick(info, source, targets, parts):
    block = targets[0].shape[1]
    for (_, carried), target in zip(bundles(parts), targets):
        for place, k in enumerate(carried):
            row = info[IDS + jnp.bitwise_xor(info[PART], k)]
            target[place] = source[pl.ds(pl.multiple_of(row * block, block), block)]


def sent_shapes(parts, block, width, dtype):
    return [pltpu.VMEM((len(carried), block, width), dtype) for _, carried in bundles(parts)]


def first_kernel(parts, info, current, x, *rest):
    sent, sem = rest[:-1], rest[-1]
    run([pltpu.make_async_copy(current, x, sem)])
    pick(info, x, sent, parts)


def first(info, current, parts, block):
    shapes = [pltpu.VMEM(current.shape, current.dtype)]
    shapes += sent_shapes(parts, block, current.shape[1], current.dtype)
    return pl.pallas_call(
        lambda *refs: first_kernel(parts, *refs),
        out_shape=shapes,
        in_specs=[SMEM, HBM],
        out_specs=[VMEM] * len(shapes),
        scratch_shapes=[pltpu.SemaphoreType.DMA],
        compiler_params=LIMIT,
    )(info, far(current))


def merge_kernel(info, col, counts, adj, own, other, fetched, total, sems):
    rows, block = adj.shape[0], adj.shape[-1]

    def fetch(row):
        return pltpu.make_async_copy(adj.at[row], fetched.at[row % 2], sems.at[row % 2])

    fetch(0).start()
    for row in range(rows):
        if row + 1 < rows:
            fetch(row + 1).start()
        total[...] = jnp.zeros_like(total)
        fetch(row).wait()

        def add(k, carry):
            entry = col[row, k]
            offset = jnp.bitwise_xor(jnp.maximum(entry - rows, 0), info[PART])
            afar = jnp.where(offset == 0, info[IDS + info[PART]], rows + offset - 1)
            total[jnp.where(entry < rows, entry, afar)] += fetched[row % 2, k].astype(jnp.float32)
            return carry

        lax.fori_loop(0, counts[row], add, 0)
        at = slice(row * block, (row + 1) * block)
        for entry in range(total.shape[0]):
            value = total[entry].astype(own.dtype)
            if entry < rows:
                own[at, entry * block : (entry + 1) * block] = value
            else:
                other[at, (entry - rows) * block : (entry - rows + 1) * block] = value


def merged(info, col, counts, adj, parts):
    rows, slots, block, _ = adj.shape
    return pl.pallas_call(
        merge_kernel,
        out_shape=[
            pltpu.VMEM((rows * block, rows * block), adj.dtype),
            pltpu.VMEM((rows * block, (parts - 1) * block), adj.dtype),
        ],
        in_specs=[SMEM, SMEM, SMEM, HBM],
        out_specs=[VMEM, VMEM],
        scratch_shapes=[
            pltpu.VMEM((2, slots, block, block), adj.dtype),
            pltpu.VMEM((rows + parts - 1, block, block), jnp.float32),
            pltpu.SemaphoreType.DMA((2,)),
        ],
        compiler_params=LIMIT,
    )(info, col, counts, far(adj))


def own_kernel(step, info, x, carried, new_h0, adj, partial, h0, sem):
    @pl.when(info[WRAPPED + step] == 1)
    def _():
        run([pltpu.make_async_copy(new_h0.at[info[SOURCE]], h0, sem)])

    @pl.when(info[WRAPPED + step] == 0)
    def _():
        run([pltpu.make_async_copy(carried, h0, sem)])

    for at in range(0, x.shape[0], TILE):
        rows = slice(at, at + TILE)
        agg = jnp.dot(adj[rows], x[...], preferred_element_type=jnp.float32)
        partial[rows] = (1.0 - teleport) * agg + teleport * h0[rows].astype(jnp.float32)


def own_part(step, info, x, carried, new_h0, adj):
    return pl.pallas_call(
        lambda *refs: own_kernel(step, *refs),
        out_shape=pltpu.VMEM(x.shape, jnp.float32),
        in_specs=[SMEM, VMEM, HBM, HBM, VMEM],
        out_specs=VMEM,
        scratch_shapes=[pltpu.VMEM(x.shape, x.dtype), pltpu.SemaphoreType.DMA],
        compiler_params=LIMIT,
    )(info, fast(x), far(carried), far(new_h0), fast(adj))


def layer_kernel(step, parts, offsets, info, beta, adj, partial, weight, new_h0, *rest):
    incoming, rest = rest[: len(offsets)], rest[len(offsets) :]
    block = incoming[0].shape[1]
    more = step < STEPS - 1
    out, following, sent = rest[0], rest[1], rest[2 : 2 + len(bundles(parts))]
    table, sem = rest[-2:]
    if more:
        fresh = pltpu.make_async_copy(new_h0.at[step], following, sem)

        @pl.when(info[STARTS + step + 1] == 1)
        def _():
            fresh.start()

    for offset, value in zip(offsets, incoming):
        table[(offset - 1) * block : offset * block] = value[0]
    scale = beta[step]
    for at in range(0, out.shape[0], TILE):
        rows = slice(at, at + TILE)
        agg = jnp.dot(adj[rows], table[...], preferred_element_type=jnp.float32)
        mixture = (partial[rows] + (1.0 - teleport) * agg).astype(jnp.bfloat16)
        product = jnp.dot(mixture, weight[...], preferred_element_type=jnp.float32)
        value = (1.0 - scale) * mixture.astype(jnp.float32) + scale * product
        out[rows] = jnp.maximum(value, 0.0).astype(out.dtype)
    if not more:
        return

    @pl.when(info[STARTS + step + 1] == 1)
    def _():
        fresh.wait()

    @pl.when(info[STARTS + step + 1] == 0)
    def _():
        following[...] = out[...]

    pick(info, following, sent, parts)


def layer(step, parts, info, beta, adj, partial, weight, new_h0, incoming, offsets):
    _, block, width = incoming[0].shape
    made = pltpu.VMEM(partial.shape, incoming[0].dtype)
    shapes = [made]
    if step < STEPS - 1:
        shapes += [made] + sent_shapes(parts, block, width, made.dtype)
    scratch = [pltpu.VMEM(((parts - 1) * block, width), made.dtype), pltpu.SemaphoreType.DMA]
    return pl.pallas_call(
        lambda *refs: layer_kernel(step, parts, offsets, *refs),
        out_shape=shapes,
        in_specs=[SMEM, SMEM, VMEM, VMEM, VMEM, HBM] + [VMEM] * len(incoming),
        out_specs=[VMEM] * len(shapes),
        scratch_shapes=scratch,
        compiler_params=LIMIT,
    )(info, beta, fast(adj), fast(partial), fast(weight), far(new_h0), *[fast(value) for value in incoming])


def keep_kernel(step, value, *rest):
    held, sem = rest[-2:]
    run([pltpu.make_async_copy(value, held.at[0, step], sem)])


def kept(step, value, held):
    return pl.pallas_call(
        lambda *refs: keep_kernel(step, *refs),
        out_shape=pltpu.HBM((1, STEPS) + value.shape, value.dtype),
        in_specs=[VMEM] if held is None else [VMEM, HBM],
        out_specs=HBM,
        scratch_shapes=[pltpu.SemaphoreType.DMA],
        input_output_aliases={} if held is None else {1: 0},
        compiler_params=LIMIT,
    )(*([fast(value)] if held is None else [fast(value), held]))


def moved(value, by):
    length = lax.axis_size("section")
    if by % length == 0:
        return value
    return lax.ppermute(value, "section", [((i + by) % length, i) for i in range(length)])


def body(carry_h, carry_h0, new_h0, weights, adj_blocks, col_index, counts, send_list):
    section = lax.axis_index("section")
    sections = lax.axis_size("section")
    part = lax.axis_index("dom")
    parts = send_list.shape[0]
    block = adj_blocks.shape[-1]
    place = section + jnp.arange(STEPS, dtype=jnp.int32)
    layers = place % sections
    beta = jnp.log(1.0 + strength / (layers.astype(jnp.float32) + 1.0))
    source = jnp.clip(sections - section - 1, 0, new_h0.shape[0] - 1)
    info = jnp.concatenate(
        [
            jnp.stack([part, source]).astype(jnp.int32),
            (place == sections).astype(jnp.int32),
            (place >= sections).astype(jnp.int32),
            lax.dynamic_index_in_dim(send_list, part, 0, keepdims=False),
        ]
    )
    current, *sent = first(info, carry_h[0], parts, block)
    layer_weights = [moved(weights[0], t) for t in range(STEPS)]
    own_adj = None
    held = None
    for t in range(STEPS):
        incoming, offsets = exchanged(sent, parts)
        if own_adj is None:
            own_adj, other_adj = merged(info, col_index, counts, adj_blocks, parts)
        partial = own_part(t, info, current, carry_h0[0], new_h0, own_adj)
        made, *rest = layer(
            t, parts, info, beta, other_adj, partial, layer_weights[t], new_h0, incoming, offsets
        )
        if rest:
            current, *sent = rest
        held = kept(t, moved(made, -t), held)
    return held


def solution(mesh):
    in_specs = (
        P("section", "dom", None),
        P("section", "dom", None),
        P(None, "dom", None),
        P("section", None, None),
        P("dom", None, None, None),
        P("dom", None),
        P("dom"),
        P(),
    )
    out_specs = P("section", None, "dom", None)
    return jax.shard_map(body, mesh=mesh, in_specs=in_specs, out_specs=out_specs, check_vma=False)
```

```python
import jax
import jax.numpy as jnp
from jax import lax
from jax.experimental import pallas as pl
from jax.experimental.pallas import tpu as pltpu
from jax.sharding import PartitionSpec as P

STEPS = 4
TILE = 512

teleport = 0.2
strength = 1.5

PART, STARTS, IDS = 0, 1, 1 + STEPS

VMEM = pl.BlockSpec(memory_space=pltpu.VMEM)
SMEM = pl.BlockSpec(memory_space=pltpu.SMEM)
HBM = pl.BlockSpec(memory_space=pltpu.HBM)
LIMIT = pltpu.CompilerParams(vmem_limit_bytes=16 * 2**20)


def fast(value):
    return pltpu.with_memory_space_constraint(value, pltpu.VMEM)


def far(value):
    return pltpu.with_memory_space_constraint(value, pltpu.HBM)


def run(copies):
    for copy in copies:
        copy.start()
    for copy in copies:
        copy.wait()


def relays(parts):
    quarter = parts // 4
    if quarter == 0:
        return {}
    hops = {}
    for k in range(2 * quarter, 3 * quarter):
        across = k - 2 * quarter
        hops[k] = (quarter + across, 3 * quarter) if across % 2 == 0 else (3 * quarter + across, quarter)
    return hops


def bundles(parts):
    via = {}
    for k, (first, _) in relays(parts).items():
        via.setdefault(first, []).append(k)
    order = sorted(via) + [k for k in range(1, parts) if k not in via and k not in relays(parts)]
    return [(hop, [hop] + via.get(hop, [])) for hop in order]


def swapped(value, offset):
    parts = lax.axis_size("dom")
    return lax.ppermute(value, "dom", [(i, i ^ offset) for i in range(parts)])


def passed_on(got, parts):
    hops = relays(parts)
    arrays, offsets = [], []
    for (_, carried), value in zip(bundles(parts), got):
        for place, k in enumerate(carried[1:], 1):
            arrays.append(swapped(value[place : place + 1], hops[k][1]))
            offsets.append(k)
    return arrays, offsets


def pick(info, source, targets, parts):
    block = targets[0].shape[1]
    for (_, carried), target in zip(bundles(parts), targets):
        for place, k in enumerate(carried):
            row = info[IDS + jnp.bitwise_xor(info[PART], k)]
            target[place] = source[pl.ds(pl.multiple_of(row * block, block), block)]


def sent_shapes(parts, block, width, dtype):
    return [pltpu.VMEM((len(carried), block, width), dtype) for _, carried in bundles(parts)]


def first_kernel(parts, info, current, carried, x, h0, *rest):
    sent, sems = rest[:-1], rest[-1]
    spans = [slice(at, at + TILE) for at in range(0, x.shape[0], TILE)]
    copies = [pltpu.make_async_copy(current.at[rows], x.at[rows], sems.at[at]) for at, rows in enumerate(spans)]
    anchor = pltpu.make_async_copy(carried, h0, sems.at[len(spans)])
    run(copies)
    anchor.start()
    pick(info, x, sent, parts)
    anchor.wait()


def first(info, current, carried, parts, block):
    shapes = [pltpu.VMEM(current.shape, current.dtype)] * 2
    shapes += sent_shapes(parts, block, current.shape[1], current.dtype)
    return pl.pallas_call(
        lambda *refs: first_kernel(parts, *refs),
        out_shape=shapes,
        in_specs=[SMEM, HBM, HBM],
        out_specs=[VMEM] * len(shapes),
        scratch_shapes=[pltpu.SemaphoreType.DMA((current.shape[0] // TILE + 1,))],
        compiler_params=LIMIT,
    )(info, far(current), far(carried))


def merge_kernel(info, col, counts, adj, own, other, fetched, total, sems):
    rows, block = adj.shape[0], adj.shape[-1]

    def fetch(row):
        return pltpu.make_async_copy(adj.at[row], fetched.at[row % 2], sems.at[row % 2])

    fetch(0).start()
    for row in range(rows):
        if row + 1 < rows:
            fetch(row + 1).start()
        total[...] = jnp.zeros_like(total)
        fetch(row).wait()

        def add(k, carry):
            entry = col[row, k]
            offset = jnp.bitwise_xor(jnp.maximum(entry - rows, 0), info[PART])
            afar = jnp.where(offset == 0, info[IDS + info[PART]], rows + offset - 1)
            total[jnp.where(entry < rows, entry, afar)] += fetched[row % 2, k].astype(jnp.float32)
            return carry

        lax.fori_loop(0, counts[row], add, 0)
        at = slice(row * block, (row + 1) * block)
        for entry in range(total.shape[0]):
            value = total[entry].astype(own.dtype)
            if entry < rows:
                own[at, entry * block : (entry + 1) * block] = value
            else:
                other[at, (entry - rows) * block : (entry - rows + 1) * block] = value


def merged(info, col, counts, adj, parts):
    rows, slots, block, _ = adj.shape
    return pl.pallas_call(
        merge_kernel,
        out_shape=[
            pltpu.VMEM((rows * block, rows * block), adj.dtype),
            pltpu.VMEM((rows * block, (parts - 1) * block), adj.dtype),
        ],
        in_specs=[SMEM, SMEM, SMEM, HBM],
        out_specs=[VMEM, VMEM],
        scratch_shapes=[
            pltpu.VMEM((2, slots, block, block), adj.dtype),
            pltpu.VMEM((rows + parts - 1, block, block), jnp.float32),
            pltpu.SemaphoreType.DMA((2,)),
        ],
        compiler_params=LIMIT,
    )(info, col, counts, far(adj))


def own_kernel(x, h0, adj, partial):
    for at in range(0, x.shape[0], TILE):
        rows = slice(at, at + TILE)
        agg = jnp.dot(adj[rows], x[...], preferred_element_type=jnp.float32)
        partial[rows] = (1.0 - teleport) * agg + teleport * h0[rows].astype(jnp.float32)


def own_part(x, h0, adj):
    return pl.pallas_call(
        own_kernel,
        out_shape=pltpu.VMEM(x.shape, jnp.float32),
        in_specs=[VMEM, VMEM, VMEM],
        out_specs=VMEM,
        compiler_params=LIMIT,
    )(fast(x), fast(h0), fast(adj))


def layer_kernel(step, parts, offsets, info, beta, adj, partial, weight, new_h0, h0, *rest):
    incoming, rest = rest[: len(offsets)], rest[len(offsets) :]
    block = incoming[0].shape[1]
    more = step < STEPS - 1
    out, following, anchor, sent = rest[0], rest[1], rest[2], rest[3 : 3 + len(bundles(parts))]
    table, sem = rest[-2:]
    if more:
        fresh = pltpu.make_async_copy(new_h0.at[step], following, sem)

        @pl.when(info[STARTS + step + 1] == 1)
        def _():
            fresh.start()

    for offset, value in zip(offsets, incoming):
        table[(offset - 1) * block : offset * block] = value[0]
    scale = beta[step]
    for at in range(0, out.shape[0], TILE):
        rows = slice(at, at + TILE)
        agg = jnp.dot(adj[rows], table[...], preferred_element_type=jnp.float32)
        mixture = (partial[rows] + (1.0 - teleport) * agg).astype(jnp.bfloat16)
        product = jnp.dot(mixture, weight[...], preferred_element_type=jnp.float32)
        value = (1.0 - scale) * mixture.astype(jnp.float32) + scale * product
        out[rows] = jnp.maximum(value, 0.0).astype(out.dtype)
    if not more:
        return

    @pl.when(info[STARTS + step + 1] == 1)
    def _():
        fresh.wait()
        anchor[...] = following[...]

    @pl.when(info[STARTS + step + 1] == 0)
    def _():
        following[...] = out[...]

    pick(info, following, sent, parts)


def layer(step, parts, info, beta, adj, partial, weight, new_h0, h0, incoming, offsets):
    _, block, width = incoming[0].shape
    made = pltpu.VMEM(partial.shape, incoming[0].dtype)
    shapes = [made]
    if step < STEPS - 1:
        shapes += [made, made] + sent_shapes(parts, block, width, made.dtype)
    scratch = [pltpu.VMEM(((parts - 1) * block, width), made.dtype), pltpu.SemaphoreType.DMA]
    return pl.pallas_call(
        lambda *refs: layer_kernel(step, parts, offsets, *refs),
        out_shape=shapes,
        in_specs=[SMEM, SMEM, VMEM, VMEM, VMEM, HBM, VMEM] + [VMEM] * len(incoming),
        out_specs=[VMEM] * len(shapes),
        scratch_shapes=scratch,
        input_output_aliases={6: 2} if step < STEPS - 1 else {},
        compiler_params=LIMIT,
    )(info, beta, fast(adj), fast(partial), fast(weight), far(new_h0), fast(h0), *[fast(value) for value in incoming])


def keep_kernel(step, value, *rest):
    held, sem = rest[-2:]
    run([pltpu.make_async_copy(value, held.at[0, step], sem)])


def kept(step, value, held):
    return pl.pallas_call(
        lambda *refs: keep_kernel(step, *refs),
        out_shape=pltpu.HBM((1, STEPS) + value.shape, value.dtype),
        in_specs=[VMEM] if held is None else [VMEM, HBM],
        out_specs=HBM,
        scratch_shapes=[pltpu.SemaphoreType.DMA],
        input_output_aliases={} if held is None else {1: 0},
        compiler_params=LIMIT,
    )(*([fast(value)] if held is None else [fast(value), held]))


def moved(value, by):
    length = lax.axis_size("section")
    if by % length == 0:
        return value
    return lax.ppermute(value, "section", [((i + by) % length, i) for i in range(length)])


def body(carry_h, carry_h0, new_h0, weights, adj_blocks, col_index, counts, send_list):
    section = lax.axis_index("section")
    sections = lax.axis_size("section")
    part = lax.axis_index("dom")
    parts = send_list.shape[0]
    block = adj_blocks.shape[-1]
    place = section + jnp.arange(STEPS, dtype=jnp.int32)
    layers = place % sections
    beta = jnp.log(1.0 + strength / (layers.astype(jnp.float32) + 1.0))
    info = jnp.concatenate(
        [
            jnp.stack([part]).astype(jnp.int32),
            (place == sections).astype(jnp.int32),
            lax.dynamic_index_in_dim(send_list, part, 0, keepdims=False),
        ]
    )
    current, h0, *sent = first(info, carry_h[0], carry_h0[0], parts, block)
    hops = [hop for hop, _ in bundles(parts)]
    weight = weights[0]
    coming = {}
    moving = {}
    for t in range(STEPS):
        got = [swapped(value, hop) for value, hop in zip(sent, hops)]
        if t == 0:
            counts, current = lax.optimization_barrier((counts, current))
            own_adj, other_adj = merged(info, col_index, counts, adj_blocks, parts)
        if t == 3:
            current, moving[1] = lax.optimization_barrier((current, moving[1]))
        partial = own_part(current, h0, own_adj)
        passing = sum(len(carried) > 1 for _, carried in bundles(parts))
        early, partial = lax.optimization_barrier((got[:passing], partial))
        got = early + got[passing:]
        passed, offsets = passed_on(got, parts)
        if t + 1 < STEPS:
            held_back, early, partial = lax.optimization_barrier((weights[0], early, partial))
            coming[t + 1] = moved(held_back, t + 1)
        if t > 0:
            moving[t - 1] = moved(made, 1 - t)
            if t == 3:
                partial, moving[t - 1] = lax.optimization_barrier((partial, moving[t - 1]))
        made, *rest = layer(t, parts, info, beta, other_adj, partial, weight, new_h0, h0, got + passed, hops + offsets)
        if rest:
            current, h0, *sent = rest
            weight = coming[t + 1]
    moving[STEPS - 1] = moved(made, 1 - STEPS)
    held = None
    for t in range(STEPS):
        held = kept(t, moving[t], held)
    return held


def solution(mesh):
    in_specs = (
        P("section", "dom", None),
        P("section", "dom", None),
        P(None, "dom", None),
        P("section", None, None),
        P("dom", None, None, None),
        P("dom", None),
        P("dom"),
        P(),
    )
    out_specs = P("section", None, "dom", None)
    return jax.shard_map(body, mesh=mesh, in_specs=in_specs, out_specs=out_specs, check_vma=False)
```

```python
import jax
import jax.numpy as jnp
from jax import lax
from jax.experimental import pallas as pl
from jax.experimental.pallas import tpu as pltpu
from jax.sharding import PartitionSpec as P

STEPS = 4
TILE = 512

teleport = 0.2
strength = 1.5

PART, STARTS, IDS = 0, 1, 1 + STEPS

VMEM = pl.BlockSpec(memory_space=pltpu.VMEM)
SMEM = pl.BlockSpec(memory_space=pltpu.SMEM)
HBM = pl.BlockSpec(memory_space=pltpu.HBM)
LIMIT = pltpu.CompilerParams(vmem_limit_bytes=16 * 2**20)


def fast(value):
    return pltpu.with_memory_space_constraint(value, pltpu.VMEM)


def far(value):
    return pltpu.with_memory_space_constraint(value, pltpu.HBM)


def run(copies):
    for copy in copies:
        copy.start()
    for copy in copies:
        copy.wait()


def relays(parts):
    quarter = parts // 4
    if quarter == 0:
        return {}
    hops = {}
    for k in range(2 * quarter, 3 * quarter):
        across = k - 2 * quarter
        hops[k] = (quarter + across, 3 * quarter) if across % 2 == 0 else (3 * quarter + across, quarter)
    return hops


def column(offset, parts):
    quarter = parts // 4
    early = parts - 1 - quarter
    late = early + offset - 2 * quarter
    return jnp.where(offset < 2 * quarter, offset - 1, jnp.where(offset < 3 * quarter, late, offset - 1 - quarter))


def bundles(parts):
    via = {}
    for k, (first, _) in relays(parts).items():
        via.setdefault(first, []).append(k)
    order = sorted(via) + [k for k in range(1, parts) if k not in via and k not in relays(parts)]
    return [(hop, [hop] + via.get(hop, [])) for hop in order]


def swapped(value, offset):
    parts = lax.axis_size("dom")
    return lax.ppermute(value, "dom", [(i, i ^ offset) for i in range(parts)])


def passed_on(got, parts):
    hops = relays(parts)
    arrays, offsets = [], []
    for (_, carried), value in zip(bundles(parts), got):
        for place, k in enumerate(carried[1:], 1):
            arrays.append(swapped(value[place : place + 1], hops[k][1]))
            offsets.append(k)
    return arrays, offsets


def pick(info, source, targets, parts):
    block = targets[0].shape[1]
    for (_, carried), target in zip(bundles(parts), targets):
        for place, k in enumerate(carried):
            row = info[IDS + jnp.bitwise_xor(info[PART], k)]
            target[place] = source[pl.ds(pl.multiple_of(row * block, block), block)]


def sent_shapes(parts, block, width, dtype):
    return [pltpu.VMEM((len(carried), block, width), dtype) for _, carried in bundles(parts)]


def first_kernel(parts, info, current, *rest):
    sent, sems = rest[:-1], rest[-1]
    block = sent[0].shape[1]
    copies = []
    for (_, carried), target in zip(bundles(parts), sent):
        for place, k in enumerate(carried):
            row = info[IDS + jnp.bitwise_xor(info[PART], k)]
            rows = pl.ds(pl.multiple_of(row * block, block), block)
            copies.append(pltpu.make_async_copy(current.at[rows], target.at[place], sems.at[k]))
    run(copies)


def first(info, current, parts, block):
    shapes = sent_shapes(parts, block, current.shape[1], current.dtype)
    return pl.pallas_call(
        lambda *refs: first_kernel(parts, *refs),
        out_shape=shapes,
        in_specs=[SMEM, HBM],
        out_specs=[VMEM] * len(shapes),
        scratch_shapes=[pltpu.SemaphoreType.DMA((parts,))],
        compiler_params=LIMIT,
    )(info, far(current))


def merge_kernel(parts, info, col, counts, adj, own, early, late, fetched, total, sems):
    rows, block = adj.shape[0], adj.shape[-1]

    def fetch(row):
        return pltpu.make_async_copy(adj.at[row], fetched.at[row % 2], sems.at[row % 2])

    fetch(0).start()
    for row in range(rows):
        if row + 1 < rows:
            fetch(row + 1).start()
        total[...] = jnp.zeros_like(total)
        fetch(row).wait()

        def add(k, carry):
            entry = col[row, k]
            offset = jnp.bitwise_xor(jnp.maximum(entry - rows, 0), info[PART])
            afar = jnp.where(offset == 0, info[IDS + info[PART]], rows + column(offset, parts))
            total[jnp.where(entry < rows, entry, afar)] += fetched[row % 2, k].astype(jnp.float32)
            return carry

        lax.fori_loop(0, counts[row], add, 0)
        at = slice(row * block, (row + 1) * block)
        for entry in range(total.shape[0]):
            value = total[entry].astype(own.dtype)
            if entry < rows:
                own[at, entry * block : (entry + 1) * block] = value
            elif (entry - rows) * block < early.shape[1]:
                early[at, (entry - rows) * block : (entry - rows + 1) * block] = value
            else:
                place = (entry - rows) * block - early.shape[1]
                late[at, place : place + block] = value


def merged(info, col, counts, adj, parts):
    rows, slots, block, _ = adj.shape
    passed = len(relays(parts))
    return pl.pallas_call(
        lambda *refs: merge_kernel(parts, *refs),
        out_shape=[
            pltpu.VMEM((rows * block, count * block), adj.dtype) for count in (rows, parts - 1 - passed, passed)
        ],
        in_specs=[SMEM, SMEM, SMEM, HBM],
        out_specs=[VMEM] * 3,
        scratch_shapes=[
            pltpu.VMEM((2, slots, block, block), adj.dtype),
            pltpu.VMEM((rows + parts - 1, block, block), jnp.float32),
            pltpu.SemaphoreType.DMA((2,)),
        ],
        compiler_params=LIMIT,
    )(info, col, counts, far(adj))


def own_kernel(x, h0, adj, partial):
    for at in range(0, x.shape[0], TILE):
        rows = slice(at, at + TILE)
        agg = jnp.dot(adj[rows], x[...], preferred_element_type=jnp.float32)
        partial[rows] = (1.0 - teleport) * agg + teleport * h0[rows].astype(jnp.float32)


def own_part(x, h0, adj):
    return pl.pallas_call(
        own_kernel,
        out_shape=pltpu.VMEM(x.shape, jnp.float32),
        in_specs=[VMEM, VMEM, VMEM],
        out_specs=VMEM,
        compiler_params=LIMIT,
    )(fast(x), fast(h0), fast(adj))


def gather_table(incoming, table):
    block = incoming[0].shape[1]
    for place, value in enumerate(incoming):
        table[place * block : (place + 1) * block] = value[0]


def arrived_kernel(adj, partial, *rest):
    incoming, added, table = rest[:-2], rest[-2], rest[-1]
    gather_table(incoming, table)
    for at in range(0, added.shape[0], TILE):
        rows = slice(at, at + TILE)
        agg = jnp.dot(adj[rows], table[...], preferred_element_type=jnp.float32)
        added[rows] = partial[rows] + (1.0 - teleport) * agg


def arrived(adj, partial, incoming):
    _, block, width = incoming[0].shape
    return pl.pallas_call(
        arrived_kernel,
        out_shape=pltpu.VMEM(partial.shape, partial.dtype),
        in_specs=[VMEM] * (2 + len(incoming)),
        out_specs=VMEM,
        scratch_shapes=[pltpu.VMEM((len(incoming) * block, width), incoming[0].dtype)],
        input_output_aliases={1: 0},
        compiler_params=LIMIT,
    )(fast(adj), fast(partial), *[fast(value) for value in incoming])


def layer_kernel(step, parts, number, info, beta, adj, partial, weight, new_h0, h0, *rest):
    incoming, rest = rest[:number], rest[number:]
    more = step < STEPS - 1
    out, following, anchor, sent = rest[0], rest[1], rest[2], rest[3 : 3 + len(bundles(parts))]
    table, sem = rest[-2:]
    if more:
        fresh = pltpu.make_async_copy(new_h0.at[step], following, sem)

        @pl.when(info[STARTS + step + 1] == 1)
        def _():
            fresh.start()

    gather_table(incoming, table)
    scale = beta[step]
    for at in range(0, out.shape[0], TILE):
        rows = slice(at, at + TILE)
        agg = jnp.dot(adj[rows], table[...], preferred_element_type=jnp.float32)
        mixture = (partial[rows] + (1.0 - teleport) * agg).astype(jnp.bfloat16)
        product = jnp.dot(mixture, weight[...], preferred_element_type=jnp.float32)
        value = (1.0 - scale) * mixture.astype(jnp.float32) + scale * product
        out[rows] = jnp.maximum(value, 0.0).astype(out.dtype)
    if not more:
        return

    @pl.when(info[STARTS + step + 1] == 1)
    def _():
        fresh.wait()
        anchor[...] = following[...]

    @pl.when(info[STARTS + step + 1] == 0)
    def _():
        following[...] = out[...]
        if step == 0:
            anchor[...] = h0[...]

    pick(info, following, sent, parts)


def layer(step, parts, info, beta, adj, partial, weight, new_h0, h0, incoming):
    _, block, width = incoming[0].shape
    made = pltpu.VMEM(partial.shape, incoming[0].dtype)
    shapes = [made]
    if step < STEPS - 1:
        shapes += [made, made] + sent_shapes(parts, block, width, made.dtype)
    scratch = [pltpu.VMEM((len(incoming) * block, width), made.dtype), pltpu.SemaphoreType.DMA]
    return pl.pallas_call(
        lambda *refs: layer_kernel(step, parts, len(incoming), *refs),
        out_shape=shapes,
        in_specs=[SMEM, SMEM, VMEM, VMEM, VMEM, HBM, VMEM] + [VMEM] * len(incoming),
        out_specs=[VMEM] * len(shapes),
        scratch_shapes=scratch,
        input_output_aliases={6: 2} if 0 < step < STEPS - 1 else {},
        compiler_params=LIMIT,
    )(info, beta, fast(adj), fast(partial), fast(weight), far(new_h0), fast(h0), *[fast(value) for value in incoming])


def keep_kernel(step, value, *rest):
    held, sem = rest[-2:]
    run([pltpu.make_async_copy(value, held.at[0, step], sem)])


def kept(step, value, held):
    return pl.pallas_call(
        lambda *refs: keep_kernel(step, *refs),
        out_shape=pltpu.HBM((1, STEPS) + value.shape, value.dtype),
        in_specs=[VMEM] if held is None else [VMEM, HBM],
        out_specs=HBM,
        scratch_shapes=[pltpu.SemaphoreType.DMA],
        input_output_aliases={} if held is None else {1: 0},
        compiler_params=LIMIT,
    )(*([fast(value)] if held is None else [fast(value), held]))


def moved(value, by):
    length = lax.axis_size("section")
    if by % length == 0:
        return value
    return lax.ppermute(value, "section", [((i + by) % length, i) for i in range(length)])


def body(carry_h, carry_h0, new_h0, weights, adj_blocks, col_index, counts, send_list):
    section = lax.axis_index("section")
    sections = lax.axis_size("section")
    part = lax.axis_index("dom")
    parts = send_list.shape[0]
    block = adj_blocks.shape[-1]
    place = section + jnp.arange(STEPS, dtype=jnp.int32)
    layers = place % sections
    beta = jnp.log(1.0 + strength / (layers.astype(jnp.float32) + 1.0))
    info = jnp.concatenate(
        [
            jnp.stack([part]).astype(jnp.int32),
            (place == sections).astype(jnp.int32),
            lax.dynamic_index_in_dim(send_list, part, 0, keepdims=False),
        ]
    )
    sent = first(info, carry_h[0], parts, block)
    current, h0 = carry_h[0], carry_h0[0]
    hops = [hop for hop, _ in bundles(parts)]
    weight = weights[0]
    coming = {}
    moving = {}
    for t in range(STEPS):
        got = [swapped(value, hop) for value, hop in zip(sent, hops)]
        if t == 0:
            counts, sent = lax.optimization_barrier((counts, sent))
            own_adj, early_adj, late_adj = merged(info, col_index, counts, adj_blocks, parts)
        if t == 3:
            current, moving[1] = lax.optimization_barrier((current, moving[1]))
        partial = own_part(current, h0, own_adj)
        passing = sum(len(carried) > 1 for _, carried in bundles(parts))
        early, partial = lax.optimization_barrier((got[:passing], partial))
        got = early + got[passing:]
        passed, offsets = passed_on(got, parts)
        if t + 1 < STEPS:
            held_back, early, partial = lax.optimization_barrier((weights[0], early, partial))
            coming[t + 1] = moved(held_back, t + 1)
        if t > 0:
            moving[t - 1] = moved(made, 1 - t)
            if t == 3:
                partial, moving[t - 1] = lax.optimization_barrier((partial, moving[t - 1]))
        partial = arrived(early_adj, partial, [value for _, value in sorted(zip(hops, got), key=lambda pair: pair[0])])
        passed = [value for _, value in sorted(zip(offsets, passed), key=lambda pair: pair[0])]
        made, *rest = layer(t, parts, info, beta, late_adj, partial, weight, new_h0, h0, passed)
        if rest:
            current, h0, *sent = rest
            weight = coming[t + 1]
    moving[STEPS - 1] = moved(made, 1 - STEPS)
    held = None
    for t in range(STEPS):
        held = kept(t, moving[t], held)
    return held


def solution(mesh):
    in_specs = (
        P("section", "dom", None),
        P("section", "dom", None),
        P(None, "dom", None),
        P("section", None, None),
        P("dom", None, None, None),
        P("dom", None),
        P("dom"),
        P(),
    )
    out_specs = P("section", None, "dom", None)
    return jax.shard_map(body, mesh=mesh, in_specs=in_specs, out_specs=out_specs, check_vma=False)
```

```python
import jax
import jax.numpy as jnp
from jax import lax
from jax.experimental import pallas as pl
from jax.experimental.pallas import tpu as pltpu
from jax.sharding import PartitionSpec as P

STEPS = 4
TILE = 512
H0_FROM, H0_BY = 0, 0
OUT1 = True

teleport = 0.2
strength = 1.5

PART, ANCHOR, STAYS, STARTS, IDS = 0, 1, 2, 3, 3 + STEPS

VMEM = pl.BlockSpec(memory_space=pltpu.VMEM)
SMEM = pl.BlockSpec(memory_space=pltpu.SMEM)
HBM = pl.BlockSpec(memory_space=pltpu.HBM)
LIMIT = pltpu.CompilerParams(vmem_limit_bytes=16 * 2**20)


def fast(value):
    return pltpu.with_memory_space_constraint(value, pltpu.VMEM)


def far(value):
    return pltpu.with_memory_space_constraint(value, pltpu.HBM)


def run(copies):
    for copy in copies:
        copy.start()
    for copy in copies:
        copy.wait()


def relays(parts):
    quarter = parts // 4
    if quarter == 0:
        return {}
    hops = {}
    for k in range(2 * quarter, 3 * quarter):
        across = k - 2 * quarter
        hops[k] = (quarter + across, 3 * quarter) if across % 2 == 0 else (3 * quarter + across, quarter)
    return hops


def column(offset, parts):
    quarter = parts // 4
    early = parts - 1 - quarter
    late = early + offset - 2 * quarter
    return jnp.where(offset < 2 * quarter, offset - 1, jnp.where(offset < 3 * quarter, late, offset - 1 - quarter))


def bundles(parts):
    via = {}
    for k, (first, _) in relays(parts).items():
        via.setdefault(first, []).append(k)
    order = sorted(via) + [k for k in range(1, parts) if k not in via and k not in relays(parts)]
    return [(hop, [hop] + via.get(hop, [])) for hop in order]


def places(sections, step):
    at = list(range(sections))
    if sections == STEPS and step == STEPS - 1:
        half = sections // 2
        at[0], at[half] = half, 0
    return at


def layers_at(sections, step):
    at = places(sections, step)
    return [(at.index(s) + step) % sections for s in range(sections)]


def swapped(value, offset):
    parts = lax.axis_size("dom")
    return lax.ppermute(value, "dom", [(i, i ^ offset) for i in range(parts)])


def crossing(value, offset, step):
    sections, parts = lax.axis_size("section"), lax.axis_size("dom")
    to = places(sections, step)
    if to == places(sections, 0):
        return swapped(value, offset)
    pairs = [(s * parts + i, to[s] * parts + (i ^ offset)) for s in range(sections) for i in range(parts)]
    return lax.ppermute(value, ("section", "dom"), pairs)


def passed_on(got, parts):
    hops = relays(parts)
    arrays, offsets = [], []
    for (_, carried), value in zip(bundles(parts), got):
        for place, k in enumerate(carried[1:], 1):
            arrays.append(swapped(value[place : place + 1], hops[k][1]))
            offsets.append(k)
    return arrays, offsets


def pick(info, source, targets, parts):
    block = targets[0].shape[1]
    for (_, carried), target in zip(bundles(parts), targets):
        for place, k in enumerate(carried):
            row = info[IDS + jnp.bitwise_xor(info[PART], k)]
            target[place] = source[pl.ds(pl.multiple_of(row * block, block), block)]


def sent_shapes(parts, block, width, dtype):
    return [pltpu.VMEM((len(carried), block, width), dtype) for _, carried in bundles(parts)]


def first_kernel(parts, info, current, *rest):
    sent, sems = rest[:-1], rest[-1]
    block = sent[0].shape[1]
    copies = []
    for (_, carried), target in zip(bundles(parts), sent):
        for place, k in enumerate(carried):
            row = info[IDS + jnp.bitwise_xor(info[PART], k)]
            rows = pl.ds(pl.multiple_of(row * block, block), block)
            copies.append(pltpu.make_async_copy(current.at[rows], target.at[place], sems.at[k]))
    run(copies)


def first(info, current, parts, block):
    shapes = sent_shapes(parts, block, current.shape[1], current.dtype)
    return pl.pallas_call(
        lambda *refs: first_kernel(parts, *refs),
        out_shape=shapes,
        in_specs=[SMEM, HBM],
        out_specs=[VMEM] * len(shapes),
        scratch_shapes=[pltpu.SemaphoreType.DMA((parts,))],
        compiler_params=LIMIT,
    )(info, far(current))


def merge_kernel(parts, info, col, counts, adj, own, early, late, fetched, total, sems):
    rows, block = adj.shape[0], adj.shape[-1]

    def fetch(row):
        return pltpu.make_async_copy(adj.at[row], fetched.at[row % 2], sems.at[row % 2])

    fetch(0).start()
    for row in range(rows):
        if row + 1 < rows:
            fetch(row + 1).start()
        total[...] = jnp.zeros_like(total)
        fetch(row).wait()

        def add(k, carry):
            entry = col[row, k]
            offset = jnp.bitwise_xor(jnp.maximum(entry - rows, 0), info[PART])
            afar = jnp.where(offset == 0, info[IDS + info[PART]], rows + column(offset, parts))
            total[jnp.where(entry < rows, entry, afar)] += fetched[row % 2, k].astype(jnp.float32)
            return carry

        lax.fori_loop(0, counts[row], add, 0)
        at = slice(row * block, (row + 1) * block)
        for entry in range(total.shape[0]):
            value = total[entry].astype(own.dtype)
            if entry < rows:
                own[at, entry * block : (entry + 1) * block] = value
            elif (entry - rows) * block < early.shape[1]:
                early[at, (entry - rows) * block : (entry - rows + 1) * block] = value
            else:
                place = (entry - rows) * block - early.shape[1]
                late[at, place : place + block] = value


def merged(info, col, counts, adj, parts):
    rows, slots, block, _ = adj.shape
    passed = len(relays(parts))
    return pl.pallas_call(
        lambda *refs: merge_kernel(parts, *refs),
        out_shape=[
            pltpu.VMEM((rows * block, count * block), adj.dtype) for count in (rows, parts - 1 - passed, passed)
        ],
        in_specs=[SMEM, SMEM, SMEM, HBM],
        out_specs=[VMEM] * 3,
        scratch_shapes=[
            pltpu.VMEM((2, slots, block, block), adj.dtype),
            pltpu.VMEM((rows + parts - 1, block, block), jnp.float32),
            pltpu.SemaphoreType.DMA((2,)),
        ],
        compiler_params=LIMIT,
    )(info, col, counts, far(adj))


def own_kernel(x, h0, adj, partial):
    for at in range(0, x.shape[0], TILE):
        rows = slice(at, at + TILE)
        agg = jnp.dot(adj[rows], x[...], preferred_element_type=jnp.float32)
        partial[rows] = (1.0 - teleport) * agg + teleport * h0[rows].astype(jnp.float32)


def own_part(x, h0, adj):
    return pl.pallas_call(
        own_kernel,
        out_shape=pltpu.VMEM(x.shape, jnp.float32),
        in_specs=[VMEM, VMEM, VMEM],
        out_specs=VMEM,
        compiler_params=LIMIT,
    )(fast(x), fast(h0), fast(adj))


def changed_kernel(fresh, info, x, kept_h0, sent_h0, new_h0, adj, partial, h0, sem):
    local = pltpu.make_async_copy(new_h0.at[fresh], h0, sem)

    @pl.when(info[ANCHOR] == 2)
    def _():
        local.start()

    spans = [slice(at, at + TILE) for at in range(0, x.shape[0], TILE)]
    for rows in spans:
        partial[rows] = (1.0 - teleport) * jnp.dot(adj[rows], x[...], preferred_element_type=jnp.float32)

    def add(source):
        for rows in spans:
            partial[rows] += teleport * source[rows].astype(jnp.float32)

    @pl.when(info[ANCHOR] == 0)
    def _():
        add(kept_h0)

    @pl.when(info[ANCHOR] == 1)
    def _():
        add(sent_h0)

    @pl.when(info[ANCHOR] == 2)
    def _():
        local.wait()
        add(h0)


def changed_part(fresh, info, x, kept_h0, sent_h0, new_h0, adj):
    return pl.pallas_call(
        lambda *refs: changed_kernel(fresh, *refs),
        out_shape=pltpu.VMEM(x.shape, jnp.float32),
        in_specs=[SMEM, VMEM, VMEM, VMEM, HBM, VMEM],
        out_specs=VMEM,
        scratch_shapes=[pltpu.VMEM(x.shape, x.dtype), pltpu.SemaphoreType.DMA],
        compiler_params=LIMIT,
    )(info, fast(x), fast(kept_h0), fast(sent_h0), far(new_h0), fast(adj))


def gather_table(incoming, table):
    block = incoming[0].shape[1]
    for place, value in enumerate(incoming):
        table[place * block : (place + 1) * block] = value[0]


def arrived_kernel(adj, partial, *rest):
    incoming, added, table = rest[:-2], rest[-2], rest[-1]
    gather_table(incoming, table)
    for at in range(0, added.shape[0], TILE):
        rows = slice(at, at + TILE)
        agg = jnp.dot(adj[rows], table[...], preferred_element_type=jnp.float32)
        added[rows] = partial[rows] + (1.0 - teleport) * agg


def arrived(adj, partial, incoming):
    _, block, width = incoming[0].shape
    return pl.pallas_call(
        arrived_kernel,
        out_shape=pltpu.VMEM(partial.shape, partial.dtype),
        in_specs=[VMEM] * (2 + len(incoming)),
        out_specs=VMEM,
        scratch_shapes=[pltpu.VMEM((len(incoming) * block, width), incoming[0].dtype)],
        input_output_aliases={1: 0},
        compiler_params=LIMIT,
    )(fast(adj), fast(partial), *[fast(value) for value in incoming])


def layer_kernel(step, parts, number, info, beta, adj, partial, weight, new_h0, h0, *rest):
    incoming, rest = rest[:number], rest[number:]
    more = step < STEPS - 1
    out, following, anchor, sent = rest[0], rest[1], rest[2], rest[3 : 3 + len(bundles(parts))]
    table, sem = rest[-2:]
    if more:
        fresh = pltpu.make_async_copy(new_h0.at[step], following, sem)

        @pl.when(info[STARTS + step + 1] == 1)
        def _():
            fresh.start()

    gather_table(incoming, table)
    scale = beta[step]
    for at in range(0, out.shape[0], TILE):
        rows = slice(at, at + TILE)
        agg = jnp.dot(adj[rows], table[...], preferred_element_type=jnp.float32)
        mixture = (partial[rows] + (1.0 - teleport) * agg).astype(jnp.bfloat16)
        product = jnp.dot(mixture, weight[...], preferred_element_type=jnp.float32)
        value = (1.0 - scale) * mixture.astype(jnp.float32) + scale * product
        out[rows] = jnp.maximum(value, 0.0).astype(out.dtype)
    if not more:
        return

    @pl.when(info[STARTS + step + 1] == 1)
    def _():
        fresh.wait()
        anchor[...] = following[...]

    @pl.when(info[STARTS + step + 1] == 0)
    def _():
        following[...] = out[...]
        if step == 0:
            anchor[...] = h0[...]

    pick(info, following, sent, parts)


def layer(step, parts, info, beta, adj, partial, weight, new_h0, h0, incoming):
    _, block, width = incoming[0].shape
    made = pltpu.VMEM(partial.shape, incoming[0].dtype)
    shapes = [made]
    if step < STEPS - 1:
        shapes += [made, made] + sent_shapes(parts, block, width, made.dtype)
    scratch = [pltpu.VMEM((len(incoming) * block, width), made.dtype), pltpu.SemaphoreType.DMA]
    return pl.pallas_call(
        lambda *refs: layer_kernel(step, parts, len(incoming), *refs),
        out_shape=shapes,
        in_specs=[SMEM, SMEM, VMEM, VMEM, VMEM, HBM, VMEM] + [VMEM] * len(incoming),
        out_specs=[VMEM] * len(shapes),
        scratch_shapes=scratch,
        input_output_aliases={6: 2} if 0 < step < STEPS - 1 else {},
        compiler_params=LIMIT,
    )(info, beta, fast(adj), fast(partial), fast(weight), far(new_h0), fast(h0), *[fast(value) for value in incoming])


def keep_kernel(step, value, *rest):
    held, sem = rest[-2:]
    run([pltpu.make_async_copy(value, held.at[0, step], sem)])


def kept(step, value, held):
    return pl.pallas_call(
        lambda *refs: keep_kernel(step, *refs),
        out_shape=pltpu.HBM((1, STEPS) + value.shape, value.dtype),
        in_specs=[VMEM] if held is None else [VMEM, HBM],
        out_specs=HBM,
        scratch_shapes=[pltpu.SemaphoreType.DMA],
        input_output_aliases={} if held is None else {1: 0},
        compiler_params=LIMIT,
    )(*([fast(value)] if held is None else [fast(value), held]))


def keep_one_kernel(step, info, first_value, second_value, _, held, sem):
    for choice, value in enumerate((first_value, second_value)):

        @pl.when(info[STAYS] == choice)
        def _():
            run([pltpu.make_async_copy(value, held.at[0, step], sem)])


def kept_one(step, info, first_value, second_value, held):
    return pl.pallas_call(
        lambda *refs: keep_one_kernel(step, *refs),
        out_shape=pltpu.HBM(held.shape, held.dtype),
        in_specs=[SMEM, VMEM, VMEM, HBM],
        out_specs=HBM,
        scratch_shapes=[pltpu.SemaphoreType.DMA],
        input_output_aliases={3: 0},
        compiler_params=LIMIT,
    )(info, fast(first_value), fast(second_value), held)


def routed(value, pairs):
    if all(source == target for source, target in pairs):
        return value
    return lax.ppermute(value, "section", pairs)


def body(carry_h, carry_h0, new_h0, weights, adj_blocks, col_index, counts, send_list):
    section = lax.axis_index("section")
    sections = lax.axis_size("section")
    part = lax.axis_index("dom")
    parts = send_list.shape[0]
    block = adj_blocks.shape[-1]
    tables = [layers_at(sections, t) for t in range(STEPS)]
    last = STEPS - 1
    at_last = places(sections, last)
    changes = at_last != places(sections, 0)
    steps = jnp.arange(STEPS, dtype=jnp.int32)
    place = section + steps
    half = sections // 2
    leaves, enters = place == steps, place == steps + half
    ahead = jnp.where(leaves, half, jnp.where(enters, -half, 0)) if changes else jnp.zeros_like(place)
    layers = (place + jnp.where(steps == last, ahead, 0)) % sections
    beta = jnp.log(1.0 + strength / (layers.astype(jnp.float32) + 1.0))
    stays = [int(at_last[s] == s) for s in range(sections)]
    info = jnp.concatenate(
        [
            part.astype(jnp.int32)[None],
            jnp.where(leaves, 2, jnp.where(enters, 1, 0))[:1],
            jnp.where(leaves | enters, 0, 1)[:1],
            (place == sections).astype(jnp.int32),
            lax.dynamic_index_in_dim(send_list, part, 0, keepdims=False),
        ]
    )
    sent = first(info, carry_h[0], parts, block)
    current, h0 = carry_h[0], carry_h0[0]
    hops = [hop for hop, _ in bundles(parts)]
    weight = weights[0]
    coming = {}
    moving = {}
    for t in range(STEPS):
        change = changes and t == last
        got = [crossing(value, hop, t) for value, hop in zip(sent, hops)]
        if t == 0:
            counts, sent = lax.optimization_barrier((counts, sent))
            own_adj, early_adj, late_adj = merged(info, col_index, counts, adj_blocks, parts)
        if t == last and not change:
            current, moving[t - 2] = lax.optimization_barrier((current, moving[t - 2]))
        passing = sum(len(carried) > 1 for _, carried in bundles(parts))
        early = got[:passing]
        if change:
            current = lax.ppermute(current, "section", [(s, at_last[s]) for s in range(sections)])
            partial = changed_part(sections // 2 - 1, info, current, h0, other_h0, new_h0, own_adj)
        else:
            partial = own_part(current, h0, own_adj)
            early, partial = lax.optimization_barrier((early, partial))
            got = early + got[passing:]
        passed, offsets = passed_on(got, parts)
        if t < last:
            held_back, early, partial = lax.optimization_barrier((weights[0], early, partial))
            coming[t + 1] = routed(held_back, [(layer_at, s) for s, layer_at in enumerate(tables[t + 1])])
        if changes and t == H0_FROM:
            other_h0 = lax.ppermute(carry_h0[0], "section", [(0, sections // 2)])
        if changes and t == H0_BY:
            partial, other_h0 = lax.optimization_barrier((partial, other_h0))
        if t > 0:
            pairs = list(enumerate(tables[t - 1]))
            if change:
                pairs = [(s, to) for s, to in pairs if stays[s]]
            moving[t - 1] = routed(made, pairs)
            if t == last and not change:
                partial, moving[t - 1] = lax.optimization_barrier((partial, moving[t - 1]))
            if change and OUT1:
                partial, moving[t - 2] = lax.optimization_barrier((partial, moving[t - 2]))
        partial = arrived(early_adj, partial, [value for _, value in sorted(zip(hops, got), key=lambda pair: pair[0])])
        passed = [value for _, value in sorted(zip(offsets, passed), key=lambda pair: pair[0])]
        made, *rest = layer(t, parts, info, beta, late_adj, partial, weight, new_h0, h0, passed)
        if rest:
            current, h0, *sent = rest
            weight = coming[t + 1]
    moving[last] = routed(made, list(enumerate(tables[last])))
    held = None
    for t in range(STEPS):
        if changes and t == last - 1:
            held = kept_one(t, info, current, moving[t], held)
        else:
            held = kept(t, moving[t], held)
    return held


def solution(mesh):
    in_specs = (
        P("section", "dom", None),
        P("section", "dom", None),
        P(None, "dom", None),
        P("section", None, None),
        P("dom", None, None, None),
        P("dom", None),
        P("dom"),
        P(),
    )
    out_specs = P("section", None, "dom", None)
    return jax.shard_map(body, mesh=mesh, in_specs=in_specs, out_specs=out_specs, check_vma=False)
```

```python
import jax
import jax.numpy as jnp
from jax import lax
from jax.experimental import pallas as pl
from jax.experimental.pallas import tpu as pltpu
from jax.sharding import PartitionSpec as P

STEPS = 4
TILE = 512
H0_FROM, H0_BY = 0, 0
OUT1 = True

teleport = 0.2
strength = 1.5

PART, ANCHOR, STAYS, STARTS, IDS = 0, 1, 2, 3, 3 + STEPS

VMEM = pl.BlockSpec(memory_space=pltpu.VMEM)
SMEM = pl.BlockSpec(memory_space=pltpu.SMEM)
HBM = pl.BlockSpec(memory_space=pltpu.HBM)
LIMIT = pltpu.CompilerParams(vmem_limit_bytes=16 * 2**20)


def fast(value):
    return pltpu.with_memory_space_constraint(value, pltpu.VMEM)


def far(value):
    return pltpu.with_memory_space_constraint(value, pltpu.HBM)


def run(copies):
    for copy in copies:
        copy.start()
    for copy in copies:
        copy.wait()


def relays(parts):
    quarter = parts // 4
    if quarter == 0:
        return {}
    hops = {}
    for k in range(2 * quarter, 3 * quarter):
        across = k - 2 * quarter
        hops[k] = (quarter + across, 3 * quarter) if across % 2 == 0 else (3 * quarter + across, quarter)
    return hops


def column(offset, parts):
    quarter = parts // 4
    early = parts - 1 - quarter
    late = early + offset - 2 * quarter
    return jnp.where(offset < 2 * quarter, offset - 1, jnp.where(offset < 3 * quarter, late, offset - 1 - quarter))


def bundles(parts):
    via = {}
    for k, (first, _) in relays(parts).items():
        via.setdefault(first, []).append(k)
    order = sorted(via) + [k for k in range(1, parts) if k not in via and k not in relays(parts)]
    return [(hop, [hop] + via.get(hop, [])) for hop in order]


def places(sections, step):
    at = list(range(sections))
    if sections == STEPS and step == STEPS - 1:
        half = sections // 2
        at[0], at[half] = half, 0
    return at


def layers_at(sections, step):
    at = places(sections, step)
    return [(at.index(s) + step) % sections for s in range(sections)]


def swapped(value, offset):
    parts = lax.axis_size("dom")
    return lax.ppermute(value, "dom", [(i, i ^ offset) for i in range(parts)])


def crossing(value, offset, step):
    sections, parts = lax.axis_size("section"), lax.axis_size("dom")
    to = places(sections, step)
    if to == places(sections, 0):
        return swapped(value, offset)
    pairs = [(s * parts + i, to[s] * parts + (i ^ offset)) for s in range(sections) for i in range(parts)]
    return lax.ppermute(value, ("section", "dom"), pairs)


def passed_on(got, parts):
    hops = relays(parts)
    arrays, offsets = [], []
    for (_, carried), value in zip(bundles(parts), got):
        for place, k in enumerate(carried[1:], 1):
            arrays.append(swapped(value[place : place + 1], hops[k][1]))
            offsets.append(k)
    return arrays, offsets


def pick(info, source, targets, parts):
    block = targets[0].shape[1]
    for (_, carried), target in zip(bundles(parts), targets):
        for place, k in enumerate(carried):
            row = info[IDS + jnp.bitwise_xor(info[PART], k)]
            target[place] = source[pl.ds(pl.multiple_of(row * block, block), block)]


def sent_shapes(parts, block, width, dtype):
    return [pltpu.VMEM((len(carried), block, width), dtype) for _, carried in bundles(parts)]


def first_kernel(parts, info, current, *rest):
    sent, sems = rest[:-1], rest[-1]
    block = sent[0].shape[1]
    copies = []
    for (_, carried), target in zip(bundles(parts), sent):
        for place, k in enumerate(carried):
            row = info[IDS + jnp.bitwise_xor(info[PART], k)]
            rows = pl.ds(pl.multiple_of(row * block, block), block)
            copies.append(pltpu.make_async_copy(current.at[rows], target.at[place], sems.at[k]))
    run(copies)


def first(info, current, parts, block):
    shapes = sent_shapes(parts, block, current.shape[1], current.dtype)
    return pl.pallas_call(
        lambda *refs: first_kernel(parts, *refs),
        out_shape=shapes,
        in_specs=[SMEM, HBM],
        out_specs=[VMEM] * len(shapes),
        scratch_shapes=[pltpu.SemaphoreType.DMA((parts,))],
        compiler_params=LIMIT,
    )(info, far(current))


def merge_kernel(parts, info, col, counts, adj, own, early, late, fetched, total, sems):
    rows, block = adj.shape[0], adj.shape[-1]

    def fetch(row):
        return pltpu.make_async_copy(adj.at[row], fetched.at[row % 2], sems.at[row % 2])

    fetch(0).start()
    for row in range(rows):
        if row + 1 < rows:
            fetch(row + 1).start()
        total[...] = jnp.zeros_like(total)
        fetch(row).wait()

        def add(k, carry):
            entry = col[row, k]
            offset = jnp.bitwise_xor(jnp.maximum(entry - rows, 0), info[PART])
            afar = jnp.where(offset == 0, info[IDS + info[PART]], rows + column(offset, parts))
            total[jnp.where(entry < rows, entry, afar)] += fetched[row % 2, k].astype(jnp.float32)
            return carry

        lax.fori_loop(0, counts[row], add, 0)
        at = slice(row * block, (row + 1) * block)
        for entry in range(total.shape[0]):
            value = total[entry].astype(own.dtype)
            if entry < rows:
                own[at, entry * block : (entry + 1) * block] = value
            elif (entry - rows) * block < early.shape[1]:
                early[at, (entry - rows) * block : (entry - rows + 1) * block] = value
            else:
                place = (entry - rows) * block - early.shape[1]
                late[at, place : place + block] = value


def merged(info, col, counts, adj, parts):
    rows, slots, block, _ = adj.shape
    passed = len(relays(parts))
    return pl.pallas_call(
        lambda *refs: merge_kernel(parts, *refs),
        out_shape=[
            pltpu.VMEM((rows * block, count * block), adj.dtype) for count in (rows, parts - 1 - passed, passed)
        ],
        in_specs=[SMEM, SMEM, SMEM, HBM],
        out_specs=[VMEM] * 3,
        scratch_shapes=[
            pltpu.VMEM((2, slots, block, block), adj.dtype),
            pltpu.VMEM((rows + parts - 1, block, block), jnp.float32),
            pltpu.SemaphoreType.DMA((2,)),
        ],
        compiler_params=LIMIT,
    )(info, col, counts, far(adj))


def own_kernel(x, h0, adj, partial):
    for at in range(0, x.shape[0], TILE):
        rows = slice(at, at + TILE)
        agg = jnp.dot(adj[rows], x[...], preferred_element_type=jnp.float32)
        partial[rows] = (1.0 - teleport) * agg + teleport * h0[rows].astype(jnp.float32)


def own_part(x, h0, adj):
    return pl.pallas_call(
        own_kernel,
        out_shape=pltpu.VMEM(x.shape, jnp.float32),
        in_specs=[VMEM, VMEM, VMEM],
        out_specs=VMEM,
        cost_estimate=pl.CostEstimate(flops=2 * adj.size * x.shape[1], bytes_accessed=0, transcendentals=0),
        compiler_params=LIMIT,
    )(fast(x), fast(h0), fast(adj))


def changed_kernel(fresh, info, x, kept_h0, sent_h0, new_h0, adj, partial, h0, sem):
    local = pltpu.make_async_copy(new_h0.at[fresh], h0, sem)

    @pl.when(info[ANCHOR] == 2)
    def _():
        local.start()

    spans = [slice(at, at + TILE) for at in range(0, x.shape[0], TILE)]
    for rows in spans:
        partial[rows] = (1.0 - teleport) * jnp.dot(adj[rows], x[...], preferred_element_type=jnp.float32)

    def add(source):
        for rows in spans:
            partial[rows] += teleport * source[rows].astype(jnp.float32)

    @pl.when(info[ANCHOR] == 0)
    def _():
        add(kept_h0)

    @pl.when(info[ANCHOR] == 1)
    def _():
        add(sent_h0)

    @pl.when(info[ANCHOR] == 2)
    def _():
        local.wait()
        add(h0)


def changed_part(fresh, info, x, kept_h0, sent_h0, new_h0, adj):
    return pl.pallas_call(
        lambda *refs: changed_kernel(fresh, *refs),
        out_shape=pltpu.VMEM(x.shape, jnp.float32),
        in_specs=[SMEM, VMEM, VMEM, VMEM, HBM, VMEM],
        out_specs=VMEM,
        scratch_shapes=[pltpu.VMEM(x.shape, x.dtype), pltpu.SemaphoreType.DMA],
        cost_estimate=pl.CostEstimate(flops=2 * adj.size * x.shape[1], bytes_accessed=0, transcendentals=0),
        compiler_params=LIMIT,
    )(info, fast(x), fast(kept_h0), fast(sent_h0), far(new_h0), fast(adj))


def gather_table(incoming, table):
    block = incoming[0].shape[1]
    for place, value in enumerate(incoming):
        table[place * block : (place + 1) * block] = value[0]


def arrived_kernel(adj, partial, *rest):
    incoming, added, table = rest[:-2], rest[-2], rest[-1]
    gather_table(incoming, table)
    for at in range(0, added.shape[0], TILE):
        rows = slice(at, at + TILE)
        agg = jnp.dot(adj[rows], table[...], preferred_element_type=jnp.float32)
        added[rows] = partial[rows] + (1.0 - teleport) * agg


def arrived(adj, partial, incoming):
    _, block, width = incoming[0].shape
    return pl.pallas_call(
        arrived_kernel,
        out_shape=pltpu.VMEM(partial.shape, partial.dtype),
        in_specs=[VMEM] * (2 + len(incoming)),
        out_specs=VMEM,
        scratch_shapes=[pltpu.VMEM((len(incoming) * block, width), incoming[0].dtype)],
        input_output_aliases={1: 0},
        cost_estimate=pl.CostEstimate(flops=2 * adj.size * partial.shape[1], bytes_accessed=0, transcendentals=0),
        compiler_params=LIMIT,
    )(fast(adj), fast(partial), *[fast(value) for value in incoming])


def layer_kernel(step, parts, number, info, beta, adj, partial, weight, new_h0, h0, *rest):
    incoming, rest = rest[:number], rest[number:]
    more = step < STEPS - 1
    out, following, anchor, sent = rest[0], rest[1], rest[2], rest[3 : 3 + len(bundles(parts))]
    table, sem = rest[-2:]
    if more:
        fresh = pltpu.make_async_copy(new_h0.at[step], following, sem)

        @pl.when(info[STARTS + step + 1] == 1)
        def _():
            fresh.start()

    gather_table(incoming, table)
    scale = beta[step]
    for at in range(0, out.shape[0], TILE):
        rows = slice(at, at + TILE)
        agg = jnp.dot(adj[rows], table[...], preferred_element_type=jnp.float32)
        mixture = (partial[rows] + (1.0 - teleport) * agg).astype(jnp.bfloat16)
        product = jnp.dot(mixture, weight[...], preferred_element_type=jnp.float32)
        value = (1.0 - scale) * mixture.astype(jnp.float32) + scale * product
        out[rows] = jnp.maximum(value, 0.0).astype(out.dtype)
    if not more:
        return

    @pl.when(info[STARTS + step + 1] == 1)
    def _():
        fresh.wait()
        anchor[...] = following[...]

    @pl.when(info[STARTS + step + 1] == 0)
    def _():
        following[...] = out[...]
        if step == 0:
            anchor[...] = h0[...]

    pick(info, following, sent, parts)


def layer(step, parts, info, beta, adj, partial, weight, new_h0, h0, incoming):
    _, block, width = incoming[0].shape
    made = pltpu.VMEM(partial.shape, incoming[0].dtype)
    shapes = [made]
    if step < STEPS - 1:
        shapes += [made, made] + sent_shapes(parts, block, width, made.dtype)
    scratch = [pltpu.VMEM((len(incoming) * block, width), made.dtype), pltpu.SemaphoreType.DMA]
    return pl.pallas_call(
        lambda *refs: layer_kernel(step, parts, len(incoming), *refs),
        out_shape=shapes,
        in_specs=[SMEM, SMEM, VMEM, VMEM, VMEM, HBM, VMEM] + [VMEM] * len(incoming),
        out_specs=[VMEM] * len(shapes),
        scratch_shapes=scratch,
        input_output_aliases={6: 2} if 0 < step < STEPS - 1 else {},
        cost_estimate=pl.CostEstimate(flops=2 * (adj.size + weight.size * 2) * partial.shape[1], bytes_accessed=0, transcendentals=0),
        compiler_params=LIMIT,
    )(info, beta, fast(adj), fast(partial), fast(weight), far(new_h0), fast(h0), *[fast(value) for value in incoming])


def keep_kernel(step, value, *rest):
    held, sem = rest[-2:]
    run([pltpu.make_async_copy(value, held.at[0, step], sem)])


def kept(step, value, held):
    return pl.pallas_call(
        lambda *refs: keep_kernel(step, *refs),
        out_shape=pltpu.HBM((1, STEPS) + value.shape, value.dtype),
        in_specs=[VMEM] if held is None else [VMEM, HBM],
        out_specs=HBM,
        scratch_shapes=[pltpu.SemaphoreType.DMA],
        input_output_aliases={} if held is None else {1: 0},
        compiler_params=LIMIT,
    )(*([fast(value)] if held is None else [fast(value), held]))


def keep_one_kernel(step, info, first_value, second_value, _, held, sem):
    for choice, value in enumerate((first_value, second_value)):

        @pl.when(info[STAYS] == choice)
        def _():
            run([pltpu.make_async_copy(value, held.at[0, step], sem)])


def kept_one(step, info, first_value, second_value, held):
    return pl.pallas_call(
        lambda *refs: keep_one_kernel(step, *refs),
        out_shape=pltpu.HBM(held.shape, held.dtype),
        in_specs=[SMEM, VMEM, VMEM, HBM],
        out_specs=HBM,
        scratch_shapes=[pltpu.SemaphoreType.DMA],
        input_output_aliases={3: 0},
        compiler_params=LIMIT,
    )(info, fast(first_value), fast(second_value), held)


def routed(value, pairs):
    if all(source == target for source, target in pairs):
        return value
    return lax.ppermute(value, "section", pairs)


def body(carry_h, carry_h0, new_h0, weights, adj_blocks, col_index, counts, send_list):
    section = lax.axis_index("section")
    sections = lax.axis_size("section")
    part = lax.axis_index("dom")
    parts = send_list.shape[0]
    block = adj_blocks.shape[-1]
    tables = [layers_at(sections, t) for t in range(STEPS)]
    last = STEPS - 1
    at_last = places(sections, last)
    changes = at_last != places(sections, 0)
    steps = jnp.arange(STEPS, dtype=jnp.int32)
    place = section + steps
    half = sections // 2
    leaves, enters = place == steps, place == steps + half
    ahead = jnp.where(leaves, half, jnp.where(enters, -half, 0)) if changes else jnp.zeros_like(place)
    layers = (place + jnp.where(steps == last, ahead, 0)) % sections
    beta = jnp.log(1.0 + strength / (layers.astype(jnp.float32) + 1.0))
    stays = [int(at_last[s] == s) for s in range(sections)]
    info = jnp.concatenate(
        [
            part.astype(jnp.int32)[None],
            jnp.where(leaves, 2, jnp.where(enters, 1, 0))[:1],
            jnp.where(leaves | enters, 0, 1)[:1],
            (place == sections).astype(jnp.int32),
            lax.dynamic_index_in_dim(send_list, part, 0, keepdims=False),
        ]
    )
    sent = first(info, carry_h[0], parts, block)
    current, h0 = carry_h[0], carry_h0[0]
    hops = [hop for hop, _ in bundles(parts)]
    weight = weights[0]
    coming = {}
    moving = {}
    for t in range(STEPS):
        change = changes and t == last
        got = [crossing(value, hop, t) for value, hop in zip(sent, hops)]
        if t == 0:
            counts, sent = lax.optimization_barrier((counts, sent))
            own_adj, early_adj, late_adj = merged(info, col_index, counts, adj_blocks, parts)
        if t == last and not change:
            current, moving[t - 2] = lax.optimization_barrier((current, moving[t - 2]))
        passing = sum(len(carried) > 1 for _, carried in bundles(parts))
        early = got[:passing]
        if change:
            current = lax.ppermute(current, "section", [(s, at_last[s]) for s in range(sections)])
            partial = changed_part(sections // 2 - 1, info, current, h0, other_h0, new_h0, own_adj)
        else:
            partial = own_part(current, h0, own_adj)
            early, partial = lax.optimization_barrier((early, partial))
            got = early + got[passing:]
        passed, offsets = passed_on(got, parts)
        if t < last:
            held_back, early, partial = lax.optimization_barrier((weights[0], early, partial))
            coming[t + 1] = routed(held_back, [(layer_at, s) for s, layer_at in enumerate(tables[t + 1])])
        if changes and t == H0_FROM:
            other_h0 = lax.ppermute(carry_h0[0], "section", [(0, sections // 2)])
        if changes and t == H0_BY:
            partial, other_h0 = lax.optimization_barrier((partial, other_h0))
        if t > 0:
            pairs = list(enumerate(tables[t - 1]))
            if change:
                pairs = [(s, to) for s, to in pairs if stays[s]]
            moving[t - 1] = routed(made, pairs)
            if t == last and not change:
                partial, moving[t - 1] = lax.optimization_barrier((partial, moving[t - 1]))
            if change and OUT1:
                partial, moving[t - 2] = lax.optimization_barrier((partial, moving[t - 2]))
        partial = arrived(early_adj, partial, [value for _, value in sorted(zip(hops, got), key=lambda pair: pair[0])])
        passed = [value for _, value in sorted(zip(offsets, passed), key=lambda pair: pair[0])]
        made, *rest = layer(t, parts, info, beta, late_adj, partial, weight, new_h0, h0, passed)
        if rest:
            current, h0, *sent = rest
            weight = coming[t + 1]
    moving[last] = routed(made, list(enumerate(tables[last])))
    held = None
    for t in range(STEPS):
        if changes and t == last - 1:
            held = kept_one(t, info, current, moving[t], held)
        else:
            held = kept(t, moving[t], held)
    return held


def solution(mesh):
    in_specs = (
        P("section", "dom", None),
        P("section", "dom", None),
        P(None, "dom", None),
        P("section", None, None),
        P("dom", None, None, None),
        P("dom", None),
        P("dom"),
        P(),
    )
    out_specs = P("section", None, "dom", None)
    return jax.shard_map(body, mesh=mesh, in_specs=in_specs, out_specs=out_specs, check_vma=False)
```
